32 devices in a mesh: sy: 4 (over z), sx: 4 (over y, core), tp: 2 (over x).
Axes of the slice: x: 2, y: 2, z: 4, core: 2. Of those that a mesh axis runs over, the one named last changes fastest.
Arguments:
- features: bfloat16 [96, 64, 1408], P('sy', 'sx', 'tp'), may hold values from -6 to 6
- depth_kernel: float32 [7, 7, 1408], P(None, None, 'tp'), may hold values from -0.875 to 0.875
- depth_bias: float32 [1408], P('tp'), may hold values from -1 to 1
- norm_gain: float32 [1408], replicated, may hold values from 0.1 to 1.9
- norm_bias: float32 [1408], replicated, may hold values from -3 to 3
- up_weight: bfloat16 [1408, 5632], P(None, 'tp'), may hold values from -0.15625 to 0.15625
- up_bias: float32 [5632], P('tp'), may hold values from -3 to 3
- response_gain: float32 [5632], P('tp'), may hold values from -4 to 4
- response_shift: float32 [5632], P('tp'), may hold values from -3 to 3
- down_weight: bfloat16 [5632, 1408], P('tp', ('sy', 'sx')), may hold values from -0.078125 to 0.078125
- down_bias: float32 [1408], P('tp'), may hold values from -3 to 3
- tissue: int32 [12, 8], P('sy', 'sx'), may hold values from 0 to 1, as said below
- cotangent: bfloat16 [96, 64, 1408], P('sy', 'sx', 'tp'), may hold values from -6 to 6
Outputs:
- block_out: bfloat16 [96, 64, 1408], P('sy', 'sx', 'tp')
- feature_grad: bfloat16 [96, 64, 1408], P('sy', 'sx', 'tp')
The draws below stay inside these ranges and needn't reach their ends.
Inputs may be any that keep to these rules, and one draw needn't show every extreme that they name: Each device's block of 3 x 2 tiles holds 1 to 4 tissue tiles; some device's block holds exactly 4.
All inputs are finite; a program needn't handle non-finite values.
Results may differ from the reference program's by a relative error of at most 0.0049.
The reference program's roundings to bfloat16 on the way (of `convolved`, `normed`, `hidden`, `response`, `masked_cot`, `preact_grad` and `convolved_grad`) count: a program that leaves them out, or rounds other values in their place, can miss the bound.
Values may be sent and summed in bfloat16 or wider, within the bound.
A program may use at most 128 MiB of HBM per device.

```python
import jax
import jax.numpy as jnp
from jax import lax

CH = 1408
HIDDEN_SIZE = 5632
KERNEL = 7
TILE = 8
TISSUE_MOST = 4
ROWS_DEV = 24
COLS_DEV = 16
IMG_ROWS = 96
IMG_COLS = 64
TILES_Y = 3
TILES_X = 2
MASK_ROWS = 12
MASK_COLS = 8


def draw_tissue(key, part):
    blocks_y = MASK_ROWS // TILES_Y
    blocks_x = MASK_COLS // TILES_X
    blocks = blocks_y * blocks_x
    per_block = TILES_Y * TILES_X
    key_count, key_full, key_rank = jax.random.split(key, 3)
    counts = jax.random.randint(key_count, (blocks,), 1, TISSUE_MOST + 1)
    chosen = jax.random.randint(key_full, (), 0, blocks)
    counts = jnp.where(jnp.arange(blocks) == chosen, TISSUE_MOST, counts)
    scores = jax.random.randint(key_rank, (blocks, per_block), 0, 1 << 20) * per_block + jnp.arange(per_block)[None, :]
    ranking = jnp.argsort(jnp.argsort(scores, axis=1), axis=1)
    tissue_flags = (ranking < counts[:, None]).astype(jnp.int32)
    return tissue_flags.reshape(blocks_y, blocks_x, TILES_Y, TILES_X).transpose(0, 2, 1, 3).reshape(MASK_ROWS, MASK_COLS)


def steps_of(stream_key, dims, cuts, smallest, largest):
    def one(position, parts):
        heights = jax.random.uniform(jax.random.fold_in(jax.random.fold_in(stream_key, 6), position), (parts,), jnp.float32, smallest / len(cuts), largest / len(cuts))
        return jnp.repeat(jnp.exp(heights), dims[position] // parts).reshape((-1,) + (1,) * (len(dims) - position - 1))

    loudness = one(*cuts[0])
    for cut in cuts[1:]:
        loudness = loudness * one(*cut)
    return loudness


def gaussian(own_key, dims, deviation, bound, cuts=(), kind=jnp.bfloat16):
    gain = steps_of(own_key, dims, cuts, -0.22, 0.18) if cuts else 1.0
    values = jax.random.normal(own_key, dims, jnp.float32) * deviation * gain
    return jnp.minimum(jnp.maximum(values, -bound), bound).astype(kind)


def setup_inputs(seed: int = 0) -> dict:
    splits = jax.random.split(jax.random.key(seed), 14)
    return {
        "features": gaussian(splits[0], (IMG_ROWS, IMG_COLS, CH), 1.0, 6.0, ((0, 4), (1, 4), (2, 2))),
        "depth_kernel": gaussian(splits[1], (KERNEL, KERNEL, CH), (KERNEL * KERNEL) ** -0.5, 0.875, ((2, 2),), jnp.float32),
        "depth_bias": jnp.clip(jax.random.uniform(splits[2], (CH,), jnp.float32, -1.0, 1.0) * steps_of(splits[2], (CH,), ((0, 2),), -0.4, 0.0), -1.0, 1.0),
        "norm_gain": jnp.clip(1.0 + 0.18 * jax.random.normal(splits[3], (CH,), jnp.float32), 0.1, 1.9),
        "norm_bias": gaussian(splits[4], (CH,), 0.5, 3.0, (), jnp.float32),
        "up_weight": gaussian(splits[5], (CH, HIDDEN_SIZE), CH ** -0.5, 0.15625, ((1, 2),)),
        "up_bias": gaussian(splits[6], (HIDDEN_SIZE,), 0.5, 3.0, ((0, 2),), jnp.float32),
        "response_gain": gaussian(splits[7], (HIDDEN_SIZE,), 1.0, 4.0, ((0, 2),), jnp.float32),
        "response_shift": gaussian(splits[8], (HIDDEN_SIZE,), 0.5, 3.0, ((0, 2),), jnp.float32),
        "down_weight": gaussian(splits[9], (HIDDEN_SIZE, CH), HIDDEN_SIZE ** -0.5, 0.078125, ((0, 2), (1, 16))),
        "down_bias": gaussian(splits[10], (CH,), 0.5, 3.0, ((0, 2),), jnp.float32),
        "tissue": draw_tissue(jax.random.fold_in(splits[13], 71), 0),
        "cotangent": gaussian(splits[12], (IMG_ROWS, IMG_COLS, CH), 1.0, 6.0, ((0, 4), (1, 4), (2, 2))),
    }


root_half = 0.7071067811865476
root_two_pi_inv = 0.3989422804014327

def gelu_value(values):
    return 0.5 * values * (1.0 + jax.scipy.special.erf(values * root_half))

def gelu_slope(values):
    return 0.5 * (1.0 + jax.scipy.special.erf(values * root_half)) + values * jnp.exp(-0.5 * values * values) * root_two_pi_inv

def depthwise(padded, kernel, rows_out, cols_out, flipped):
    summed = jnp.zeros((rows_out, cols_out, kernel.shape[2]), jnp.float32)
    last_tap = KERNEL - 1
    for row_tap in range(KERNEL):
        for col_tap in range(KERNEL):
            row_start = last_tap - row_tap if flipped else row_tap
            col_start = last_tap - col_tap if flipped else col_tap
            window = padded[row_start:row_start + rows_out, col_start:col_start + cols_out]
            summed = summed + window.astype(jnp.float32) * kernel[row_tap, col_tap]
    return summed

def reference(features, depth_kernel, depth_bias, norm_gain, norm_bias, up_weight, up_bias, response_gain, response_shift, down_weight, down_bias, tissue, cotangent):
    image_rows, image_cols, channels = features.shape
    hidden_count = up_weight.shape[1]
    halo_width = KERNEL // 2
    pixel_count = image_rows * image_cols
    pixel_mask = jnp.repeat(jnp.repeat(tissue, TILE, axis=0), TILE, axis=1).astype(jnp.float32)
    padded = jnp.pad(features, ((halo_width, halo_width), (halo_width, halo_width), (0, 0)))
    convolved = (depthwise(padded, depth_kernel, image_rows, image_cols, False) + depth_bias).astype(jnp.bfloat16)
    conv_rows = convolved.reshape(pixel_count, channels).astype(jnp.float32)
    centre = lax.optimization_barrier(jnp.mean(conv_rows, axis=1, keepdims=True))
    spread = lax.optimization_barrier(jnp.mean(jnp.square(conv_rows - centre), axis=1, keepdims=True))
    inv_scale = lax.rsqrt(spread + 1e-06)
    standard = (conv_rows - centre) * inv_scale
    normed = (standard * norm_gain + norm_bias).astype(jnp.bfloat16)
    mask_rows = pixel_mask.reshape(pixel_count)
    masked_cot = (cotangent.reshape(pixel_count, channels).astype(jnp.float32) * mask_rows[:, None]).astype(jnp.bfloat16)
    block_rows = ROWS_DEV * COLS_DEV
    blocks = pixel_count // block_rows

    def first_pass(running, inputs):
        normed_block, cotangent_rows, mask_block = inputs
        preact = jnp.dot(normed_block, up_weight, preferred_element_type=jnp.float32) + up_bias
        hidden = lax.optimization_barrier(gelu_value(preact).astype(jnp.bfloat16)).astype(jnp.float32)
        back_hidden = jnp.dot(cotangent_rows, down_weight.T, preferred_element_type=jnp.float32)
        squares, products = running
        squares = squares + lax.optimization_barrier(jnp.sum(mask_block[:, None] * hidden * hidden, axis=0))
        products = products + lax.optimization_barrier(jnp.sum(back_hidden * hidden, axis=0))
        return ((squares, products), (preact, back_hidden))
    empty_sums = jnp.zeros((hidden_count,), jnp.float32)
    stacked = (normed.reshape(blocks, block_rows, channels), masked_cot.reshape(blocks, block_rows, channels), mask_rows.reshape(blocks, block_rows))
    (squares, products), (preact_all, back_all) = lax.scan(first_pass, (empty_sums, empty_sums), stacked)
    column_norms = jnp.sqrt(squares)
    norm_level = jnp.mean(column_norms) + 1e-06
    norm_ratio = column_norms / norm_level
    ratio_grad = response_gain * products
    norms_grad = ratio_grad / norm_level - jnp.sum(ratio_grad * column_norms) / (hidden_count * norm_level * norm_level)

    def second_pass(running, inputs):
        preact, back_hidden, mask_block = inputs
        hidden = lax.optimization_barrier(gelu_value(preact).astype(jnp.bfloat16)).astype(jnp.float32)
        response = (response_gain * hidden * norm_ratio + response_shift + hidden).astype(jnp.bfloat16)
        branch = jnp.dot(response, down_weight, preferred_element_type=jnp.float32)
        hidden_grad = back_hidden * (response_gain * norm_ratio + 1.0) + norms_grad * mask_block[:, None] * hidden / column_norms
        preact_grad = (hidden_grad * gelu_slope(preact)).astype(jnp.bfloat16)
        normed_grad = jnp.dot(preact_grad, up_weight.T, preferred_element_type=jnp.float32)
        return (running, (branch, normed_grad))
    _, (branch_all, normed_grad_all) = lax.scan(second_pass, jnp.zeros((), jnp.float32), (preact_all, back_all, mask_rows.reshape(blocks, block_rows)))
    branch_image = branch_all.reshape(image_rows, image_cols, channels)
    block_out = (features.astype(jnp.float32) + pixel_mask[:, :, None] * (branch_image + down_bias)).astype(jnp.bfloat16)
    scaled = normed_grad_all.reshape(pixel_count, channels) * norm_gain
    convolved_grad = inv_scale * (scaled - lax.optimization_barrier(jnp.mean(scaled, axis=1, keepdims=True)) - standard * lax.optimization_barrier(jnp.mean(scaled * standard, axis=1, keepdims=True)))
    convolved_grad = convolved_grad.astype(jnp.bfloat16).reshape(image_rows, image_cols, channels)
    grad_padded = jnp.pad(convolved_grad, ((halo_width, halo_width), (halo_width, halo_width), (0, 0)))
    feature_grad = (cotangent.astype(jnp.float32) + depthwise(grad_padded, depth_kernel, image_rows, image_cols, True)).astype(jnp.bfloat16)
    return (block_out, feature_grad)
```

```python
import jax
import jax.numpy as jnp
from jax import lax
from jax.sharding import PartitionSpec as P

KERNEL = 7
TILE = 8


root_half = 0.7071067811865476
root_two_pi_inv = 0.3989422804014327


def extended(block, sides, width):
    for axis, dim in sides:
        count = lax.axis_size(axis)
        forward = [(i, i + 1) for i in range(count - 1)]
        backward = [(target, source) for source, target in forward]
        low = lax.ppermute(
            lax.slice_in_dim(block, block.shape[dim] - width, None, axis=dim), axis, forward
        )
        high = lax.ppermute(lax.slice_in_dim(block, 0, width, axis=dim), axis, backward)
        block = jnp.concatenate([low, block, high], axis=dim)
    return block


def gelu_value(values):
    return 0.5 * values * (1.0 + jax.scipy.special.erf(values * root_half))


def gelu_slope(values):
    return (
        0.5 * (1.0 + jax.scipy.special.erf(values * root_half))
        + values * jnp.exp(-0.5 * values * values) * root_two_pi_inv
    )


def depthwise(padded, kernel, rows_out, cols_out, flipped):
    summed = jnp.zeros((rows_out, cols_out, kernel.shape[2]), jnp.float32)
    last_tap = KERNEL - 1
    for row_tap in range(KERNEL):
        for col_tap in range(KERNEL):
            row_start = last_tap - row_tap if flipped else row_tap
            col_start = last_tap - col_tap if flipped else col_tap
            window = padded[row_start : row_start + rows_out, col_start : col_start + cols_out]
            summed = summed + window.astype(jnp.float32) * kernel[row_tap, col_tap]
    return summed


MOST = 4


def extend(image):
    return extended(image, (("sy", 0), ("sx", 1)), KERNEL // 2)


def swapped(array):
    count = lax.axis_size("tp")
    return lax.ppermute(array, "tp", [(i, count - 1 - i) for i in range(count)])


def over_pixels(vector):
    return lax.psum(vector, ("sy", "sx"))


def conv_tiles(windows, kernel):
    summed = jnp.zeros((windows.shape[0], TILE, TILE, windows.shape[3]), jnp.float32)
    for row_tap in range(KERNEL):
        for col_tap in range(KERNEL):
            window = windows[:, row_tap : row_tap + TILE, col_tap : col_tap + TILE]
            summed = summed + window.astype(jnp.float32) * kernel[row_tap, col_tap]
    return summed


def shards(
    features,
    depth_kernel,
    depth_bias,
    norm_gain,
    norm_bias,
    up_weight,
    up_bias,
    response_gain,
    response_shift,
    down_weight,
    down_bias,
    tissue,
    cotangent,
):
    image_rows, image_cols, local_channels = features.shape
    tiles_y, tiles_x = tissue.shape
    tiles = tiles_y * tiles_x
    channels = up_weight.shape[0]
    hidden_total = up_weight.shape[1] * lax.axis_size("tp")
    tp_index = lax.axis_index("tp")
    first = tp_index == 0
    channel_start = tp_index * local_channels
    other_start = (1 - tp_index) * local_channels
    contract_last = (((1,), (1,)), ((), ()))
    pixels = MOST * TILE * TILE

    down_t = lax.all_gather(down_weight.T, ("sy", "sx"), axis=0, tiled=True)

    flags = tissue.reshape(-1)
    tile_ids = jnp.arange(tiles, dtype=jnp.int32)
    earlier = (tile_ids[None, :] < tile_ids[:, None]).astype(jnp.int32)
    ahead = jnp.sum(earlier * flags[None, :], axis=1)
    slot_of = jnp.where(flags > 0, ahead, jnp.sum(flags) + tile_ids - ahead)
    chosen = [jnp.sum(jnp.where(slot_of == s, tile_ids, 0)) for s in range(MOST)]
    slot_mask = jnp.stack([jnp.sum(jnp.where(slot_of == s, flags, 0)) for s in range(MOST)])
    mask_rows = jnp.repeat(slot_mask, TILE * TILE).astype(jnp.float32)

    def windows_of(image, side):
        return jnp.stack(
            [
                lax.dynamic_slice(
                    image,
                    ((t // tiles_x) * TILE, (t % tiles_x) * TILE, 0),
                    (side, side, image.shape[2]),
                )
                for t in chosen
            ]
        )

    def spread_out(rows_array):
        held = rows_array.reshape(MOST, TILE, TILE, rows_array.shape[1])
        held = jnp.concatenate([held, jnp.zeros_like(held[:1])], axis=0)
        slots = jnp.minimum(slot_of, MOST)
        rows = []
        for ty in range(tiles_y):
            row = [
                lax.dynamic_index_in_dim(held, slots[ty * tiles_x + tx], 0, keepdims=False)
                for tx in range(tiles_x)
            ]
            rows.append(jnp.concatenate(row, axis=1))
        return jnp.concatenate(rows, axis=0)

    def both_halves(own):
        other = swapped(own)
        return jnp.where(
            first,
            jnp.concatenate([own, other], axis=1),
            jnp.concatenate([other, own], axis=1),
        )

    cot_tiles = windows_of(cotangent, TILE).reshape(pixels, local_channels)
    masked_cot = (cot_tiles.astype(jnp.float32) * mask_rows[:, None]).astype(jnp.bfloat16)
    cot_wide = both_halves(masked_cot)

    convolved = conv_tiles(windows_of(extend(features), TILE + KERNEL - 1), depth_kernel)
    convolved = (convolved + depth_bias).astype(jnp.bfloat16).reshape(pixels, local_channels)
    gathered = both_halves(convolved).astype(jnp.float32)
    centre = jnp.mean(gathered, axis=1, keepdims=True)
    spread = jnp.mean(jnp.square(gathered - centre), axis=1, keepdims=True)
    inv_scale = lax.rsqrt(spread + 1e-06)
    standard = (gathered - centre) * inv_scale
    normed = (standard * norm_gain + norm_bias).astype(jnp.bfloat16)
    preact = jnp.dot(normed, up_weight, preferred_element_type=jnp.float32) + up_bias
    hidden = gelu_value(preact).astype(jnp.bfloat16)
    hidden_wide = hidden.astype(jnp.float32)
    squares = over_pixels(jnp.sum(mask_rows[:, None] * hidden_wide * hidden_wide, axis=0))
    column_norms = jnp.sqrt(squares)
    norms_here = jnp.full((8, 128), jnp.sum(column_norms))
    norm_level = (norms_here + swapped(norms_here))[0, 0] / hidden_total + 1e-06
    norm_ratio = column_norms / norm_level

    back_hidden = jnp.dot(cot_wide, down_t, preferred_element_type=jnp.float32)
    products = over_pixels(jnp.sum(back_hidden * hidden_wide, axis=0))

    response = (response_gain * hidden_wide * norm_ratio + response_shift + hidden_wide).astype(
        jnp.bfloat16
    )
    partial_out = lax.dot_general(
        response, down_t, contract_last, preferred_element_type=jnp.float32
    )
    sent_out = lax.dynamic_slice_in_dim(partial_out, other_start, local_channels, 1)
    kept_out = lax.dynamic_slice_in_dim(partial_out, channel_start, local_channels, 1)
    branch = kept_out + swapped(sent_out.astype(jnp.bfloat16)).astype(jnp.float32)

    ratio_grad = response_gain * products
    dots_here = jnp.full((8, 128), jnp.sum(ratio_grad * column_norms))
    dots = (dots_here + swapped(dots_here))[0, 0]
    norms_grad = ratio_grad / norm_level - dots / (hidden_total * norm_level * norm_level)
    hidden_grad = (
        back_hidden * (response_gain * norm_ratio + 1.0)
        + norms_grad * mask_rows[:, None] * hidden_wide / column_norms
    )
    preact_grad = (hidden_grad * gelu_slope(preact)).astype(jnp.bfloat16)
    grad_terms = lax.dot_general(
        preact_grad, up_weight, contract_last, preferred_element_type=jnp.float32
    )
    scaled_terms = grad_terms * norm_gain
    sums_here = jnp.stack(
        [jnp.sum(scaled_terms, axis=1), jnp.sum(scaled_terms * standard, axis=1)]
    )
    sums = sums_here + swapped(sums_here)
    sent_grad = lax.dynamic_slice_in_dim(scaled_terms, other_start, local_channels, 1)
    kept_grad = lax.dynamic_slice_in_dim(scaled_terms, channel_start, local_channels, 1)
    own_standard = lax.dynamic_slice_in_dim(standard, channel_start, local_channels, 1)
    scaled = kept_grad + swapped(sent_grad.astype(jnp.bfloat16)).astype(jnp.float32)
    convolved_grad = inv_scale * (
        scaled - (sums[0] / channels)[:, None] - own_standard * (sums[1] / channels)[:, None]
    )
    grad_image = spread_out(convolved_grad.astype(jnp.bfloat16))
    feature_grad = (
        cotangent.astype(jnp.float32)
        + depthwise(extend(grad_image), depth_kernel, image_rows, image_cols, True)
    ).astype(jnp.bfloat16)

    addend = spread_out(mask_rows[:, None] * (branch + down_bias))
    block_out = (features.astype(jnp.float32) + addend).astype(jnp.bfloat16)
    return (block_out, feature_grad)


def solution(mesh):
    placed = (
        P("sy", "sx", "tp"),
        P(None, None, "tp"),
        P("tp"),
        P(),
        P(),
        P(None, "tp"),
        P("tp"),
        P("tp"),
        P("tp"),
        P("tp", ("sy", "sx")),
        P("tp"),
        P("sy", "sx"),
        P("sy", "sx", "tp"),
    )
    return jax.shard_map(
        shards,
        mesh=mesh,
        in_specs=placed,
        out_specs=(P("sy", "sx", "tp"), P("sy", "sx", "tp")),
        check_vma=False,
    )
```

```python
import functools

import jax
import jax.numpy as jnp
from jax import lax
from jax.experimental import pallas as pl
from jax.experimental.pallas import tpu as pltpu
from jax.sharding import PartitionSpec as P

KERNEL = 7
TILE = 8


root_half = 0.7071067811865476
root_two_pi_inv = 0.3989422804014327


def extended(block, sides, width):
    for axis, dim in sides:
        count = lax.axis_size(axis)
        forward = [(i, i + 1) for i in range(count - 1)]
        backward = [(target, source) for source, target in forward]
        low = lax.ppermute(
            lax.slice_in_dim(block, block.shape[dim] - width, None, axis=dim), axis, forward
        )
        high = lax.ppermute(lax.slice_in_dim(block, 0, width, axis=dim), axis, backward)
        block = jnp.concatenate([low, block, high], axis=dim)
    return block


def gelu_value(values):
    return 0.5 * values * (1.0 + jax.scipy.special.erf(values * root_half))


def gelu_slope(values):
    return (
        0.5 * (1.0 + jax.scipy.special.erf(values * root_half))
        + values * jnp.exp(-0.5 * values * values) * root_two_pi_inv
    )


def depthwise(padded, kernel, rows_out, cols_out, flipped):
    summed = jnp.zeros((rows_out, cols_out, kernel.shape[2]), jnp.float32)
    last_tap = KERNEL - 1
    for row_tap in range(KERNEL):
        for col_tap in range(KERNEL):
            row_start = last_tap - row_tap if flipped else row_tap
            col_start = last_tap - col_tap if flipped else col_tap
            window = padded[row_start : row_start + rows_out, col_start : col_start + cols_out]
            summed = summed + window.astype(jnp.float32) * kernel[row_tap, col_tap]
    return summed


MOST = 4


def extend(image):
    return extended(image, (("sy", 0), ("sx", 1)), KERNEL // 2)


def swapped(array):
    count = lax.axis_size("tp")
    return lax.ppermute(array, "tp", [(i, count - 1 - i) for i in range(count)])


def conv_tiles(windows, kernel):
    summed = jnp.zeros((windows.shape[0], TILE, TILE, windows.shape[3]), jnp.float32)
    for row_tap in range(KERNEL):
        for col_tap in range(KERNEL):
            window = windows[:, row_tap : row_tap + TILE, col_tap : col_tap + TILE]
            summed = summed + window.astype(jnp.float32) * kernel[row_tap, col_tap]
    return summed


MESH = pl.DeviceIdType.MESH


def peers_of(axis, count):
    me = lax.axis_index(axis)
    return [lax.rem(me + step, count) for step in range(1, count)]


def send_round(source, slots, axis, peers, send_sems, recv_sems):
    copies = []
    for step, peer in enumerate(peers):
        copy = pltpu.make_async_remote_copy(
            src_ref=source,
            dst_ref=slots.at[step],
            send_sem=send_sems.at[step],
            recv_sem=recv_sems.at[step],
            device_id={axis: peer},
            device_id_type=MESH,
        )
        copy.start()
        copies.append(copy)
    return copies


def sums_kernel(
    sx_count,
    sy_count,
    vector_ref,
    gain_ref,
    scale_ref,
    slope_ref,
    sx_slots,
    total,
    sy_slots,
    pair,
    pair_slot,
    sx_send,
    sx_recv,
    sy_send,
    sy_recv,
    tp_send,
    tp_recv,
):
    width = gain_ref.shape[1]
    units = 2 * width
    sx_peers = peers_of("sx", sx_count)
    sy_peers = peers_of("sy", sy_count)
    tp_peer = 1 - lax.axis_index("tp")
    barrier = pltpu.get_barrier_semaphore()
    for axis, peers in (("sx", sx_peers), ("sy", sy_peers), ("tp", [tp_peer])):
        for peer in peers:
            pl.semaphore_signal(barrier, inc=1, device_id={axis: peer}, device_id_type=MESH)
    pl.semaphore_wait(barrier, len(sx_peers) + len(sy_peers) + 1)

    copies = send_round(vector_ref, sx_slots, "sx", sx_peers, sx_send, sx_recv)
    summed = vector_ref[...]
    for step, copy in enumerate(copies):
        copy.wait()
        summed = summed + sx_slots[step]
    total[...] = summed
    copies = send_round(total, sy_slots, "sy", sy_peers, sy_send, sy_recv)
    for step, copy in enumerate(copies):
        copy.wait()
        summed = summed + sy_slots[step]
    norms = jnp.sqrt(summed[:, :width])
    ratio_grad = gain_ref[...] * summed[:, width:]
    norms_sum = jnp.sum(norms, axis=1, keepdims=True)
    dots_sum = jnp.sum(ratio_grad * norms, axis=1, keepdims=True)
    pair[:, :128] = jnp.broadcast_to(norms_sum, (1, 128))
    pair[:, 128:] = jnp.broadcast_to(dots_sum, (1, 128))
    copy = pltpu.make_async_remote_copy(
        src_ref=pair,
        dst_ref=pair_slot,
        send_sem=tp_send,
        recv_sem=tp_recv,
        device_id={"tp": tp_peer},
        device_id_type=MESH,
    )
    copy.start()
    copy.wait()
    level = (pair[:, :1] + pair_slot[:, :1]) / units + 1e-06
    dots = pair[:, 128:129] + pair_slot[:, 128:129]
    scale_ref[...] = gain_ref[...] * (norms / level) + 1.0
    slope_ref[...] = (ratio_grad / level - dots / (units * level * level)) / norms


def response_scales(squares, products, gain):
    width = gain.shape[0]
    sx_count = lax.axis_size("sx")
    sy_count = lax.axis_size("sy")
    scale, slope = pl.pallas_call(
        functools.partial(sums_kernel, sx_count, sy_count),
        out_shape=[jax.ShapeDtypeStruct((1, width), jnp.float32)] * 2,
        in_specs=[pl.BlockSpec(memory_space=pltpu.VMEM)] * 2,
        out_specs=[pl.BlockSpec(memory_space=pltpu.VMEM)] * 2,
        scratch_shapes=[
            pltpu.VMEM((sx_count - 1, 1, 2 * width), jnp.float32),
            pltpu.VMEM((1, 2 * width), jnp.float32),
            pltpu.VMEM((sy_count - 1, 1, 2 * width), jnp.float32),
            pltpu.VMEM((1, 256), jnp.float32),
            pltpu.VMEM((1, 256), jnp.float32),
            pltpu.SemaphoreType.DMA((sx_count - 1,)),
            pltpu.SemaphoreType.DMA((sx_count - 1,)),
            pltpu.SemaphoreType.DMA((sy_count - 1,)),
            pltpu.SemaphoreType.DMA((sy_count - 1,)),
            pltpu.SemaphoreType.DMA,
            pltpu.SemaphoreType.DMA,
        ],
        compiler_params=pltpu.CompilerParams(collective_id=0, has_side_effects=True),
    )(jnp.concatenate([squares, products])[None], gain[None])
    return scale, slope


def shards(
    features,
    depth_kernel,
    depth_bias,
    norm_gain,
    norm_bias,
    up_weight,
    up_bias,
    response_gain,
    response_shift,
    down_weight,
    down_bias,
    tissue,
    cotangent,
):
    image_rows, image_cols, local_channels = features.shape
    tiles_y, tiles_x = tissue.shape
    tiles = tiles_y * tiles_x
    channels = up_weight.shape[0]
    tp_index = lax.axis_index("tp")
    first = tp_index == 0
    channel_start = tp_index * local_channels
    other_start = (1 - tp_index) * local_channels
    contract_last = (((1,), (1,)), ((), ()))
    pixels = MOST * TILE * TILE

    down_t = lax.all_gather(down_weight.T, ("sy", "sx"), axis=0, tiled=True)

    flags = tissue.reshape(-1)
    tile_ids = jnp.arange(tiles, dtype=jnp.int32)
    earlier = (tile_ids[None, :] < tile_ids[:, None]).astype(jnp.int32)
    ahead = jnp.sum(earlier * flags[None, :], axis=1)
    slot_of = jnp.where(flags > 0, ahead, jnp.sum(flags) + tile_ids - ahead)
    chosen = [jnp.sum(jnp.where(slot_of == s, tile_ids, 0)) for s in range(MOST)]
    slot_mask = jnp.stack([jnp.sum(jnp.where(slot_of == s, flags, 0)) for s in range(MOST)])
    mask_rows = jnp.repeat(slot_mask, TILE * TILE).astype(jnp.float32)

    def windows_of(image, side):
        return jnp.stack(
            [
                lax.dynamic_slice(
                    image,
                    ((t // tiles_x) * TILE, (t % tiles_x) * TILE, 0),
                    (side, side, image.shape[2]),
                )
                for t in chosen
            ]
        )

    def spread_out(rows_array):
        held = rows_array.reshape(MOST, TILE, TILE, rows_array.shape[1])
        held = jnp.concatenate([held, jnp.zeros_like(held[:1])], axis=0)
        slots = jnp.minimum(slot_of, MOST)
        rows = []
        for ty in range(tiles_y):
            row = [
                lax.dynamic_index_in_dim(held, slots[ty * tiles_x + tx], 0, keepdims=False)
                for tx in range(tiles_x)
            ]
            rows.append(jnp.concatenate(row, axis=1))
        return jnp.concatenate(rows, axis=0)

    def both_halves(own):
        other = swapped(own)
        return jnp.where(
            first,
            jnp.concatenate([own, other], axis=1),
            jnp.concatenate([other, own], axis=1),
        )

    cot_tiles = windows_of(cotangent, TILE).reshape(pixels, local_channels)
    masked_cot = (cot_tiles.astype(jnp.float32) * mask_rows[:, None]).astype(jnp.bfloat16)
    cot_wide = both_halves(masked_cot)

    convolved = conv_tiles(windows_of(extend(features), TILE + KERNEL - 1), depth_kernel)
    convolved = (convolved + depth_bias).astype(jnp.bfloat16).reshape(pixels, local_channels)
    gathered = both_halves(convolved).astype(jnp.float32)
    centre = jnp.mean(gathered, axis=1, keepdims=True)
    spread = jnp.mean(jnp.square(gathered - centre), axis=1, keepdims=True)
    inv_scale = lax.rsqrt(spread + 1e-06)
    standard = (gathered - centre) * inv_scale
    normed = (standard * norm_gain + norm_bias).astype(jnp.bfloat16)
    preact = jnp.dot(normed, up_weight, preferred_element_type=jnp.float32) + up_bias
    hidden = gelu_value(preact).astype(jnp.bfloat16)
    hidden_wide = hidden.astype(jnp.float32)
    squares = jnp.sum(mask_rows[:, None] * hidden_wide * hidden_wide, axis=0)

    back_hidden = jnp.dot(cot_wide, down_t, preferred_element_type=jnp.float32)
    products = jnp.sum(back_hidden * hidden_wide, axis=0)
    scale, slope = response_scales(squares, products, response_gain)

    response = (hidden_wide * scale + response_shift).astype(jnp.bfloat16)
    partial_out = lax.dot_general(
        response, down_t, contract_last, preferred_element_type=jnp.float32
    )
    sent_out = lax.dynamic_slice_in_dim(partial_out, other_start, local_channels, 1)
    kept_out = lax.dynamic_slice_in_dim(partial_out, channel_start, local_channels, 1)
    branch = kept_out + swapped(sent_out.astype(jnp.bfloat16)).astype(jnp.float32)

    hidden_grad = back_hidden * scale + slope * mask_rows[:, None] * hidden_wide
    preact_grad = (hidden_grad * gelu_slope(preact)).astype(jnp.bfloat16)
    grad_terms = lax.dot_general(
        preact_grad, up_weight, contract_last, preferred_element_type=jnp.float32
    )
    scaled_terms = grad_terms * norm_gain
    sums_here = jnp.stack(
        [jnp.sum(scaled_terms, axis=1), jnp.sum(scaled_terms * standard, axis=1)]
    )
    sums = sums_here + swapped(sums_here)
    sent_grad = lax.dynamic_slice_in_dim(scaled_terms, other_start, local_channels, 1)
    kept_grad = lax.dynamic_slice_in_dim(scaled_terms, channel_start, local_channels, 1)
    own_standard = lax.dynamic_slice_in_dim(standard, channel_start, local_channels, 1)
    scaled = kept_grad + swapped(sent_grad.astype(jnp.bfloat16)).astype(jnp.float32)
    convolved_grad = inv_scale * (
        scaled - (sums[0] / channels)[:, None] - own_standard * (sums[1] / channels)[:, None]
    )
    grad_image = spread_out(convolved_grad.astype(jnp.bfloat16))
    feature_grad = (
        cotangent.astype(jnp.float32)
        + depthwise(extend(grad_image), depth_kernel, image_rows, image_cols, True)
    ).astype(jnp.bfloat16)

    addend = spread_out(mask_rows[:, None] * (branch + down_bias))
    block_out = (features.astype(jnp.float32) + addend).astype(jnp.bfloat16)
    return (block_out, feature_grad)


def solution(mesh):
    placed = (
        P("sy", "sx", "tp"),
        P(None, None, "tp"),
        P("tp"),
        P(),
        P(),
        P(None, "tp"),
        P("tp"),
        P("tp"),
        P("tp"),
        P("tp", ("sy", "sx")),
        P("tp"),
        P("sy", "sx"),
        P("sy", "sx", "tp"),
    )
    return jax.shard_map(
        shards,
        mesh=mesh,
        in_specs=placed,
        out_specs=(P("sy", "sx", "tp"), P("sy", "sx", "tp")),
        check_vma=False,
    )
```

```python
import functools

import jax
import jax.numpy as jnp
from jax import lax
from jax.experimental import pallas as pl
from jax.experimental.pallas import tpu as pltpu
from jax.sharding import PartitionSpec as P

KERNEL = 7
TILE = 8


root_half = 0.7071067811865476
root_two_pi_inv = 0.3989422804014327


def gelu_value(values):
    return 0.5 * values * (1.0 + jax.scipy.special.erf(values * root_half))


def gelu_slope(values):
    return (
        0.5 * (1.0 + jax.scipy.special.erf(values * root_half))
        + values * jnp.exp(-0.5 * values * values) * root_two_pi_inv
    )


MOST = 4


def swapped(array):
    count = lax.axis_size("tp")
    return lax.ppermute(array, "tp", [(i, count - 1 - i) for i in range(count)])


MESH = pl.DeviceIdType.MESH


def peers_of(axis, count):
    me = lax.axis_index(axis)
    return [lax.rem(me + step, count) for step in range(1, count)]


def send_round(source, slots, axis, peers, send_sems, recv_sems):
    copies = []
    for step, peer in enumerate(peers):
        copy = pltpu.make_async_remote_copy(
            src_ref=source,
            dst_ref=slots.at[step],
            send_sem=send_sems.at[step],
            recv_sem=recv_sems.at[step],
            device_id={axis: peer},
            device_id_type=MESH,
        )
        copy.start()
        copies.append(copy)
    return copies


def sums_kernel(
    sx_count,
    sy_count,
    vector_ref,
    gain_ref,
    scale_ref,
    slope_ref,
    sx_slots,
    total,
    sy_slots,
    pair,
    pair_slot,
    sx_send,
    sx_recv,
    sy_send,
    sy_recv,
    tp_send,
    tp_recv,
):
    width = gain_ref.shape[1]
    units = 2 * width
    sx_peers = peers_of("sx", sx_count)
    sy_peers = peers_of("sy", sy_count)
    tp_peer = 1 - lax.axis_index("tp")
    barrier = pltpu.get_barrier_semaphore()
    for axis, peers in (("sx", sx_peers), ("sy", sy_peers), ("tp", [tp_peer])):
        for peer in peers:
            pl.semaphore_signal(barrier, inc=1, device_id={axis: peer}, device_id_type=MESH)
    pl.semaphore_wait(barrier, len(sx_peers) + len(sy_peers) + 1)

    copies = send_round(vector_ref, sx_slots, "sx", sx_peers, sx_send, sx_recv)
    summed = vector_ref[...]
    for step, copy in enumerate(copies):
        copy.wait()
        summed = summed + sx_slots[step]
    total[...] = summed
    copies = send_round(total, sy_slots, "sy", sy_peers, sy_send, sy_recv)
    for step, copy in enumerate(copies):
        copy.wait()
        summed = summed + sy_slots[step]
    norms = jnp.sqrt(summed[:, :width])
    ratio_grad = gain_ref[...] * summed[:, width:]
    norms_sum = jnp.sum(norms, axis=1, keepdims=True)
    dots_sum = jnp.sum(ratio_grad * norms, axis=1, keepdims=True)
    pair[:, :128] = jnp.broadcast_to(norms_sum, (1, 128))
    pair[:, 128:] = jnp.broadcast_to(dots_sum, (1, 128))
    copy = pltpu.make_async_remote_copy(
        src_ref=pair,
        dst_ref=pair_slot,
        send_sem=tp_send,
        recv_sem=tp_recv,
        device_id={"tp": tp_peer},
        device_id_type=MESH,
    )
    copy.start()
    copy.wait()
    level = (pair[:, :1] + pair_slot[:, :1]) / units + 1e-06
    dots = pair[:, 128:129] + pair_slot[:, 128:129]
    scale_ref[...] = gain_ref[...] * (norms / level) + 1.0
    slope_ref[...] = (ratio_grad / level - dots / (units * level * level)) / norms


def response_scales(squares, products, gain):
    width = gain.shape[0]
    sx_count = lax.axis_size("sx")
    sy_count = lax.axis_size("sy")
    scale, slope = pl.pallas_call(
        functools.partial(sums_kernel, sx_count, sy_count),
        out_shape=[jax.ShapeDtypeStruct((1, width), jnp.float32)] * 2,
        in_specs=[pl.BlockSpec(memory_space=pltpu.VMEM)] * 2,
        out_specs=[pl.BlockSpec(memory_space=pltpu.VMEM)] * 2,
        scratch_shapes=[
            pltpu.VMEM((sx_count - 1, 1, 2 * width), jnp.float32),
            pltpu.VMEM((1, 2 * width), jnp.float32),
            pltpu.VMEM((sy_count - 1, 1, 2 * width), jnp.float32),
            pltpu.VMEM((1, 256), jnp.float32),
            pltpu.VMEM((1, 256), jnp.float32),
            pltpu.SemaphoreType.DMA((sx_count - 1,)),
            pltpu.SemaphoreType.DMA((sx_count - 1,)),
            pltpu.SemaphoreType.DMA((sy_count - 1,)),
            pltpu.SemaphoreType.DMA((sy_count - 1,)),
            pltpu.SemaphoreType.DMA,
            pltpu.SemaphoreType.DMA,
        ],
        compiler_params=pltpu.CompilerParams(collective_id=0, has_side_effects=True),
    )(jnp.concatenate([squares, products])[None], gain[None])
    return scale, slope


REACH = KERNEL // 2
LEFT = 8
LANES = 128


def halo_kernel(
    sy_count, sx_count, image, strips, sides, ends, corners, send_sems, recv_sems
):
    rows = image.shape[0]
    deep = strips.shape[1]
    sy = lax.axis_index("sy")
    sx = lax.axis_index("sx")
    plan = []
    for dy in (-1, 0, 1):
        for dx in (-1, 0, 1):
            if dy == 0 and dx == 0:
                continue
            to_y, to_x = sy + dy, sx + dx
            there = (to_y >= 0) & (to_y < sy_count) & (to_x >= 0) & (to_x < sx_count)
            from_y, from_x = sy - dy, sx - dx
            comes = (from_y >= 0) & (from_y < sy_count) & (from_x >= 0) & (from_x < sx_count)
            strip = 0 if dx < 0 else 1
            if dy == 0:
                source, target = strips.at[strip], sides.at[1 - strip]
            elif dx == 0:
                source = image.at[pl.ds(0 if dy < 0 else rows - REACH, REACH)]
                target = ends.at[1 if dy < 0 else 0]
            else:
                source = strips.at[strip, pl.ds(0 if dy < 0 else deep - 16, 16)]
                target = corners.at[(2 if dy < 0 else 0) + (1 - strip)]
            plan.append((there, comes, {"sy": to_y, "sx": to_x}, source, target))
    barrier = pltpu.get_barrier_semaphore()
    for there, _, place, _, _ in plan:

        @pl.when(there)
        def _(place=place):
            pl.semaphore_signal(barrier, inc=1, device_id=place, device_id_type=MESH)

    pl.semaphore_wait(barrier, sum(there.astype(jnp.int32) for there, _, _, _, _ in plan))

    copies = []
    for number, (there, _, place, source, target) in enumerate(plan):
        copy = pltpu.make_async_remote_copy(
            src_ref=source,
            dst_ref=target,
            send_sem=send_sems.at[number],
            recv_sem=recv_sems.at[number],
            device_id=place,
            device_id_type=MESH,
        )
        copies.append(copy)

        @pl.when(there)
        def _(copy=copy):
            copy.start()

    for (there, comes, _, _, target), copy in zip(plan, copies):

        @pl.when(comes)
        def _(copy=copy):
            copy.wait_recv()

        @pl.when(jnp.logical_not(comes))
        def _(target=target):
            target[...] = jnp.zeros(target.shape, target.dtype)

        @pl.when(there)
        def _(copy=copy):
            copy.wait_send()


def halo(image, number):
    rows, cols, width = image.shape
    strips = jnp.stack([image[:, :REACH], image[:, cols - REACH :]])
    strips = jnp.pad(strips.reshape(2, rows * REACH, width), ((0, 0), (7, 1), (0, 0)))
    sy_count = lax.axis_size("sy")
    sx_count = lax.axis_size("sx")
    vmem = pl.BlockSpec(memory_space=pltpu.VMEM)
    return pl.pallas_call(
        functools.partial(halo_kernel, sy_count, sx_count),
        out_shape=[
            jax.ShapeDtypeStruct(strips.shape, image.dtype),
            jax.ShapeDtypeStruct((2, REACH, cols, width), image.dtype),
            jax.ShapeDtypeStruct((4, 16, width), image.dtype),
        ],
        in_specs=[vmem, vmem],
        out_specs=[vmem, vmem, vmem],
        scratch_shapes=[pltpu.SemaphoreType.DMA((8,)), pltpu.SemaphoreType.DMA((8,))],
        compiler_params=pltpu.CompilerParams(collective_id=number, has_side_effects=True),
    )(image, strips)


def conv_kernel(flipped, image, sides, ends, corners, kernel, extra, out, padded):
    rows, cols, width = image.shape
    wide = jnp.float32
    padded[REACH : REACH + rows, LEFT : LEFT + cols, :] = image[...].astype(wide)
    for end in range(2):
        at = 0 if end == 0 else REACH + rows
        padded[at : at + REACH, LEFT : LEFT + cols, :] = ends[end].astype(wide)
    for side in range(2):
        at = LEFT - REACH if side == 0 else LEFT + cols
        strip = sides[side].astype(wide)
        for row in range(rows):
            first = 7 + REACH * row
            padded[REACH + row, at : at + REACH, :] = strip[first : first + REACH]
        for end in range(2):
            corner = corners[end * 2 + side].astype(wide)
            base = 6 if end == 0 else 7
            for row in range(REACH):
                top = row if end == 0 else REACH + rows + row
                first = base + REACH * row
                padded[top, at : at + REACH, :] = corner[first : first + REACH]

    def block(step, carry):
        top = step * TILE
        for lane in range(0, width, LANES):
            lanes = slice(lane, min(lane + LANES, width))
            for col in range(0, cols, TILE):
                total = None
                for q in range(KERNEL):
                    start = col + q + LEFT - REACH
                    window = padded[pl.ds(top, TILE + KERNEL - 1), start : start + TILE, lanes]
                    for p in range(KERNEL):
                        a, b = (KERNEL - 1 - p, KERNEL - 1 - q) if flipped else (p, q)
                        term = window[p : p + TILE] * kernel[a, b : b + 1, lanes]
                        total = term if total is None else total + term
                if flipped:
                    total = total + extra[pl.ds(top, TILE), col : col + TILE, lanes].astype(wide)
                else:
                    total = total + extra[:, lanes]
                out[pl.ds(top, TILE), col : col + TILE, lanes] = total.astype(out.dtype)
        return carry

    lax.fori_loop(0, rows // TILE, block, 0)


def convolve(image, kernel, extra, flipped, number):
    rows, cols, width = image.shape
    sides, ends, corners = halo(image, number)
    vmem = pl.BlockSpec(memory_space=pltpu.VMEM)
    return pl.pallas_call(
        functools.partial(conv_kernel, flipped),
        out_shape=jax.ShapeDtypeStruct(image.shape, jnp.bfloat16),
        in_specs=[vmem] * 6,
        out_specs=vmem,
        scratch_shapes=[pltpu.VMEM((rows + KERNEL - 1, cols + 2 * LEFT, width), jnp.float32)],
        compiler_params=pltpu.CompilerParams(vmem_limit_bytes=32 * 1024 * 1024),
    )(image, sides, ends, corners, kernel, extra)


def shards(
    features,
    depth_kernel,
    depth_bias,
    norm_gain,
    norm_bias,
    up_weight,
    up_bias,
    response_gain,
    response_shift,
    down_weight,
    down_bias,
    tissue,
    cotangent,
):
    image_rows, image_cols, local_channels = features.shape
    tiles_y, tiles_x = tissue.shape
    tiles = tiles_y * tiles_x
    channels = up_weight.shape[0]
    tp_index = lax.axis_index("tp")
    first = tp_index == 0
    channel_start = tp_index * local_channels
    other_start = (1 - tp_index) * local_channels
    contract_last = (((1,), (1,)), ((), ()))
    pixels = MOST * TILE * TILE

    down_t = lax.all_gather(down_weight.T, ("sy", "sx"), axis=0, tiled=True)

    flags = tissue.reshape(-1)
    tile_ids = jnp.arange(tiles, dtype=jnp.int32)
    earlier = (tile_ids[None, :] < tile_ids[:, None]).astype(jnp.int32)
    ahead = jnp.sum(earlier * flags[None, :], axis=1)
    slot_of = jnp.where(flags > 0, ahead, jnp.sum(flags) + tile_ids - ahead)
    chosen = [jnp.sum(jnp.where(slot_of == s, tile_ids, 0)) for s in range(MOST)]
    slot_mask = jnp.stack([jnp.sum(jnp.where(slot_of == s, flags, 0)) for s in range(MOST)])
    mask_rows = jnp.repeat(slot_mask, TILE * TILE).astype(jnp.float32)

    def windows_of(image, side):
        return jnp.stack(
            [
                lax.dynamic_slice(
                    image,
                    ((t // tiles_x) * TILE, (t % tiles_x) * TILE, 0),
                    (side, side, image.shape[2]),
                )
                for t in chosen
            ]
        )

    def spread_out(rows_array):
        held = rows_array.reshape(MOST, TILE, TILE, rows_array.shape[1])
        held = jnp.concatenate([held, jnp.zeros_like(held[:1])], axis=0)
        slots = jnp.minimum(slot_of, MOST)
        rows = []
        for ty in range(tiles_y):
            row = [
                lax.dynamic_index_in_dim(held, slots[ty * tiles_x + tx], 0, keepdims=False)
                for tx in range(tiles_x)
            ]
            rows.append(jnp.concatenate(row, axis=1))
        return jnp.concatenate(rows, axis=0)

    def both_halves(own):
        other = swapped(own)
        return jnp.where(
            first,
            jnp.concatenate([own, other], axis=1),
            jnp.concatenate([other, own], axis=1),
        )

    cot_tiles = windows_of(cotangent, TILE).reshape(pixels, local_channels)
    masked_cot = (cot_tiles.astype(jnp.float32) * mask_rows[:, None]).astype(jnp.bfloat16)
    cot_wide = both_halves(masked_cot)

    convolved = convolve(features, depth_kernel, depth_bias[None], False, 1)
    convolved = windows_of(convolved, TILE).reshape(pixels, local_channels)
    gathered = both_halves(convolved).astype(jnp.float32)
    centre = jnp.mean(gathered, axis=1, keepdims=True)
    spread = jnp.mean(jnp.square(gathered - centre), axis=1, keepdims=True)
    inv_scale = lax.rsqrt(spread + 1e-06)
    standard = (gathered - centre) * inv_scale
    normed = (standard * norm_gain + norm_bias).astype(jnp.bfloat16)
    preact = jnp.dot(normed, up_weight, preferred_element_type=jnp.float32) + up_bias
    hidden = gelu_value(preact).astype(jnp.bfloat16)
    hidden_wide = hidden.astype(jnp.float32)
    squares = jnp.sum(mask_rows[:, None] * hidden_wide * hidden_wide, axis=0)

    back_hidden = jnp.dot(cot_wide, down_t, preferred_element_type=jnp.float32)
    products = jnp.sum(back_hidden * hidden_wide, axis=0)
    scale, slope = response_scales(squares, products, response_gain)

    response = (hidden_wide * scale + response_shift).astype(jnp.bfloat16)
    partial_out = lax.dot_general(
        response, down_t, contract_last, preferred_element_type=jnp.float32
    )
    sent_out = lax.dynamic_slice_in_dim(partial_out, other_start, local_channels, 1)
    kept_out = lax.dynamic_slice_in_dim(partial_out, channel_start, local_channels, 1)
    branch = kept_out + swapped(sent_out.astype(jnp.bfloat16)).astype(jnp.float32)

    hidden_grad = back_hidden * scale + slope * mask_rows[:, None] * hidden_wide
    preact_grad = (hidden_grad * gelu_slope(preact)).astype(jnp.bfloat16)
    grad_terms = lax.dot_general(
        preact_grad, up_weight, contract_last, preferred_element_type=jnp.float32
    )
    scaled_terms = grad_terms * norm_gain
    sums_here = jnp.stack(
        [jnp.sum(scaled_terms, axis=1), jnp.sum(scaled_terms * standard, axis=1)]
    )
    sums = sums_here + swapped(sums_here)
    sent_grad = lax.dynamic_slice_in_dim(scaled_terms, other_start, local_channels, 1)
    kept_grad = lax.dynamic_slice_in_dim(scaled_terms, channel_start, local_channels, 1)
    own_standard = lax.dynamic_slice_in_dim(standard, channel_start, local_channels, 1)
    scaled = kept_grad + swapped(sent_grad.astype(jnp.bfloat16)).astype(jnp.float32)
    convolved_grad = inv_scale * (
        scaled - (sums[0] / channels)[:, None] - own_standard * (sums[1] / channels)[:, None]
    )
    grad_image = spread_out(convolved_grad.astype(jnp.bfloat16))
    feature_grad = convolve(grad_image, depth_kernel, cotangent, True, 2)

    addend = spread_out(mask_rows[:, None] * (branch + down_bias))
    block_out = (features.astype(jnp.float32) + addend).astype(jnp.bfloat16)
    return (block_out, feature_grad)


def solution(mesh):
    placed = (
        P("sy", "sx", "tp"),
        P(None, None, "tp"),
        P("tp"),
        P(),
        P(),
        P(None, "tp"),
        P("tp"),
        P("tp"),
        P("tp"),
        P("tp", ("sy", "sx")),
        P("tp"),
        P("sy", "sx"),
        P("sy", "sx", "tp"),
    )
    return jax.shard_map(
        shards,
        mesh=mesh,
        in_specs=placed,
        out_specs=(P("sy", "sx", "tp"), P("sy", "sx", "tp")),
        check_vma=False,
    )
```

```python
import functools

import jax
import jax.numpy as jnp
from jax import lax
from jax.experimental import pallas as pl
from jax.experimental.pallas import tpu as pltpu
from jax.sharding import PartitionSpec as P

KERNEL = 7
TILE = 8


root_half = 0.7071067811865476
root_two_pi_inv = 0.3989422804014327


def gelu_value(values):
    return 0.5 * values * (1.0 + jax.scipy.special.erf(values * root_half))


def gelu_slope(values):
    return (
        0.5 * (1.0 + jax.scipy.special.erf(values * root_half))
        + values * jnp.exp(-0.5 * values * values) * root_two_pi_inv
    )


MOST = 4


def swapped(array):
    count = lax.axis_size("tp")
    return lax.ppermute(array, "tp", [(i, count - 1 - i) for i in range(count)])


MESH = pl.DeviceIdType.MESH


def peers_of(axis, count):
    me = lax.axis_index(axis)
    return [lax.rem(me + step, count) for step in range(1, count)]


def send_round(source, slots, axis, peers, send_sems, recv_sems):
    copies = []
    for step, peer in enumerate(peers):
        copy = pltpu.make_async_remote_copy(
            src_ref=source,
            dst_ref=slots.at[step],
            send_sem=send_sems.at[step],
            recv_sem=recv_sems.at[step],
            device_id={axis: peer},
            device_id_type=MESH,
        )
        copy.start()
        copies.append(copy)
    return copies


def sums_kernel(
    sx_count,
    sy_count,
    vector_ref,
    gain_ref,
    scale_ref,
    slope_ref,
    sx_slots,
    total,
    sy_slots,
    pair,
    pair_slot,
    sx_send,
    sx_recv,
    sy_send,
    sy_recv,
    tp_send,
    tp_recv,
):
    width = gain_ref.shape[1]
    units = 2 * width
    sx_peers = peers_of("sx", sx_count)
    sy_peers = peers_of("sy", sy_count)
    tp_peer = 1 - lax.axis_index("tp")
    barrier = pltpu.get_barrier_semaphore()
    for axis, peers in (("sx", sx_peers), ("sy", sy_peers), ("tp", [tp_peer])):
        for peer in peers:
            pl.semaphore_signal(barrier, inc=1, device_id={axis: peer}, device_id_type=MESH)
    pl.semaphore_wait(barrier, len(sx_peers) + len(sy_peers) + 1)

    copies = send_round(vector_ref, sx_slots, "sx", sx_peers, sx_send, sx_recv)
    summed = vector_ref[...]
    for step, copy in enumerate(copies):
        copy.wait()
        summed = summed + sx_slots[step]
    total[...] = summed
    copies = send_round(total, sy_slots, "sy", sy_peers, sy_send, sy_recv)
    for step, copy in enumerate(copies):
        copy.wait()
        summed = summed + sy_slots[step]
    norms = jnp.sqrt(summed[:, :width])
    ratio_grad = gain_ref[...] * summed[:, width:]
    norms_sum = jnp.sum(norms, axis=1, keepdims=True)
    dots_sum = jnp.sum(ratio_grad * norms, axis=1, keepdims=True)
    pair[:, :128] = jnp.broadcast_to(norms_sum, (1, 128))
    pair[:, 128:] = jnp.broadcast_to(dots_sum, (1, 128))
    copy = pltpu.make_async_remote_copy(
        src_ref=pair,
        dst_ref=pair_slot,
        send_sem=tp_send,
        recv_sem=tp_recv,
        device_id={"tp": tp_peer},
        device_id_type=MESH,
    )
    copy.start()
    copy.wait()
    level = (pair[:, :1] + pair_slot[:, :1]) / units + 1e-06
    dots = pair[:, 128:129] + pair_slot[:, 128:129]
    scale_ref[...] = gain_ref[...] * (norms / level) + 1.0
    slope_ref[...] = (ratio_grad / level - dots / (units * level * level)) / norms


def response_scales(squares, products, gain):
    width = gain.shape[0]
    sx_count = lax.axis_size("sx")
    sy_count = lax.axis_size("sy")
    scale, slope = pl.pallas_call(
        functools.partial(sums_kernel, sx_count, sy_count),
        out_shape=[jax.ShapeDtypeStruct((1, width), jnp.float32)] * 2,
        in_specs=[pl.BlockSpec(memory_space=pltpu.VMEM)] * 2,
        out_specs=[pl.BlockSpec(memory_space=pltpu.VMEM)] * 2,
        scratch_shapes=[
            pltpu.VMEM((sx_count - 1, 1, 2 * width), jnp.float32),
            pltpu.VMEM((1, 2 * width), jnp.float32),
            pltpu.VMEM((sy_count - 1, 1, 2 * width), jnp.float32),
            pltpu.VMEM((1, 256), jnp.float32),
            pltpu.VMEM((1, 256), jnp.float32),
            pltpu.SemaphoreType.DMA((sx_count - 1,)),
            pltpu.SemaphoreType.DMA((sx_count - 1,)),
            pltpu.SemaphoreType.DMA((sy_count - 1,)),
            pltpu.SemaphoreType.DMA((sy_count - 1,)),
            pltpu.SemaphoreType.DMA,
            pltpu.SemaphoreType.DMA,
        ],
        compiler_params=pltpu.CompilerParams(collective_id=0, has_side_effects=True),
    )(jnp.concatenate([squares, products])[None], gain[None])
    return scale, slope


REACH = KERNEL // 2
LEFT = 8
LANES = 128


def halo_kernel(
    sy_count, sx_count, image, strips, sides, ends, corners, send_sems, recv_sems
):
    rows = image.shape[0]
    deep = strips.shape[1]
    sy = lax.axis_index("sy")
    sx = lax.axis_index("sx")
    plan = []
    for dy in (-1, 0, 1):
        for dx in (-1, 0, 1):
            if dy == 0 and dx == 0:
                continue
            to_y, to_x = sy + dy, sx + dx
            there = (to_y >= 0) & (to_y < sy_count) & (to_x >= 0) & (to_x < sx_count)
            from_y, from_x = sy - dy, sx - dx
            comes = (from_y >= 0) & (from_y < sy_count) & (from_x >= 0) & (from_x < sx_count)
            strip = 0 if dx < 0 else 1
            if dy == 0:
                source, target = strips.at[strip], sides.at[1 - strip]
            elif dx == 0:
                source = image.at[pl.ds(0 if dy < 0 else rows - REACH, REACH)]
                target = ends.at[1 if dy < 0 else 0]
            else:
                source = strips.at[strip, pl.ds(0 if dy < 0 else deep - 16, 16)]
                target = corners.at[(2 if dy < 0 else 0) + (1 - strip)]
            plan.append((there, comes, {"sy": to_y, "sx": to_x}, source, target))
    barrier = pltpu.get_barrier_semaphore()
    for there, _, place, _, _ in plan:

        @pl.when(there)
        def _(place=place):
            pl.semaphore_signal(barrier, inc=1, device_id=place, device_id_type=MESH)

    pl.semaphore_wait(barrier, sum(there.astype(jnp.int32) for there, _, _, _, _ in plan))

    copies = []
    for number, (there, _, place, source, target) in enumerate(plan):
        copy = pltpu.make_async_remote_copy(
            src_ref=source,
            dst_ref=target,
            send_sem=send_sems.at[number],
            recv_sem=recv_sems.at[number],
            device_id=place,
            device_id_type=MESH,
        )
        copies.append(copy)

        @pl.when(there)
        def _(copy=copy):
            copy.start()

    for (there, comes, _, _, target), copy in zip(plan, copies):

        @pl.when(comes)
        def _(copy=copy):
            copy.wait_recv()

        @pl.when(jnp.logical_not(comes))
        def _(target=target):
            target[...] = jnp.zeros(target.shape, target.dtype)

        @pl.when(there)
        def _(copy=copy):
            copy.wait_send()


def halo(image, number):
    rows, cols, width = image.shape
    strips = jnp.stack([image[:, :REACH], image[:, cols - REACH :]])
    strips = jnp.pad(strips.reshape(2, rows * REACH, width), ((0, 0), (7, 1), (0, 0)))
    sy_count = lax.axis_size("sy")
    sx_count = lax.axis_size("sx")
    vmem = pl.BlockSpec(memory_space=pltpu.VMEM)
    return pl.pallas_call(
        functools.partial(halo_kernel, sy_count, sx_count),
        out_shape=[
            jax.ShapeDtypeStruct(strips.shape, image.dtype),
            jax.ShapeDtypeStruct((2, REACH, cols, width), image.dtype),
            jax.ShapeDtypeStruct((4, 16, width), image.dtype),
        ],
        in_specs=[vmem, vmem],
        out_specs=[vmem, vmem, vmem],
        scratch_shapes=[pltpu.SemaphoreType.DMA((8,)), pltpu.SemaphoreType.DMA((8,))],
        compiler_params=pltpu.CompilerParams(collective_id=number, has_side_effects=True),
    )(image, strips)


def conv_kernel(flipped, image, sides, ends, corners, kernel, extra, out, padded):
    rows, cols, width = image.shape
    wide = jnp.float32
    padded[REACH : REACH + rows, LEFT : LEFT + cols, :] = image[...].astype(wide)
    for end in range(2):
        at = 0 if end == 0 else REACH + rows
        padded[at : at + REACH, LEFT : LEFT + cols, :] = ends[end].astype(wide)
    for side in range(2):
        at = LEFT - REACH if side == 0 else LEFT + cols
        strip = sides[side].astype(wide)
        for row in range(rows):
            first = 7 + REACH * row
            padded[REACH + row, at : at + REACH, :] = strip[first : first + REACH]
        for end in range(2):
            corner = corners[end * 2 + side].astype(wide)
            base = 6 if end == 0 else 7
            for row in range(REACH):
                top = row if end == 0 else REACH + rows + row
                first = base + REACH * row
                padded[top, at : at + REACH, :] = corner[first : first + REACH]

    def block(step, carry):
        top = step * TILE
        for lane in range(0, width, LANES):
            lanes = slice(lane, min(lane + LANES, width))
            for col in range(0, cols, TILE):
                total = None
                for q in range(KERNEL):
                    start = col + q + LEFT - REACH
                    window = padded[pl.ds(top, TILE + KERNEL - 1), start : start + TILE, lanes]
                    for p in range(KERNEL):
                        a, b = (KERNEL - 1 - p, KERNEL - 1 - q) if flipped else (p, q)
                        term = window[p : p + TILE] * kernel[a, b : b + 1, lanes]
                        total = term if total is None else total + term
                if flipped:
                    total = total + extra[pl.ds(top, TILE), col : col + TILE, lanes].astype(wide)
                else:
                    total = total + extra[:, lanes]
                out[pl.ds(top, TILE), col : col + TILE, lanes] = total.astype(out.dtype)
        return carry

    lax.fori_loop(0, rows // TILE, block, 0)


def convolve(image, kernel, extra, flipped, number):
    rows, cols, width = image.shape
    sides, ends, corners = halo(image, number)
    vmem = pl.BlockSpec(memory_space=pltpu.VMEM)
    return pl.pallas_call(
        functools.partial(conv_kernel, flipped),
        out_shape=jax.ShapeDtypeStruct(image.shape, jnp.bfloat16),
        in_specs=[vmem] * 6,
        out_specs=vmem,
        scratch_shapes=[pltpu.VMEM((rows + KERNEL - 1, cols + 2 * LEFT, width), jnp.float32)],
        compiler_params=pltpu.CompilerParams(vmem_limit_bytes=32 * 1024 * 1024),
    )(image, sides, ends, corners, kernel, extra)


def gradient_conv(image, kernel, cotangent, sent):
    rows, cols, width = image.shape
    sides, ends, corners = halo(image, 2)
    sides, sent = lax.optimization_barrier((sides, sent))
    came = swapped(sent)
    sides = sides[:, 7 : 7 + REACH * rows].reshape(2, rows, REACH, width)
    above = corners[:2, 6:15].reshape(2, REACH, REACH, width)
    below = corners[2:, 7:16].reshape(2, REACH, REACH, width)
    columns = [
        jnp.concatenate([above[0], sides[0], below[0]], axis=0),
        jnp.concatenate([ends[0], image, ends[1]], axis=0),
        jnp.concatenate([above[1], sides[1], below[1]], axis=0),
    ]
    padded = jnp.concatenate(columns, axis=1)
    side = TILE + KERNEL - 1
    windows = jnp.stack(
        [
            padded[row : row + side, col : col + side]
            for row in range(0, rows, TILE)
            for col in range(0, cols, TILE)
        ]
    )
    summed = jnp.zeros((windows.shape[0], TILE, TILE, width), jnp.float32)
    last_tap = KERNEL - 1
    for row_tap in range(KERNEL):
        for col_tap in range(KERNEL):
            window = windows[:, row_tap : row_tap + TILE, col_tap : col_tap + TILE]
            summed = summed + window.astype(jnp.float32) * kernel[
                last_tap - row_tap, last_tap - col_tap
            ]
    summed = summed.reshape(rows // TILE, cols // TILE, TILE, TILE, width)
    summed = summed.transpose(0, 2, 1, 3, 4).reshape(rows, cols, width)
    return (cotangent.astype(jnp.float32) + summed).astype(jnp.bfloat16), came


def shards(
    features,
    depth_kernel,
    depth_bias,
    norm_gain,
    norm_bias,
    up_weight,
    up_bias,
    response_gain,
    response_shift,
    down_weight,
    down_bias,
    tissue,
    cotangent,
):
    image_rows, image_cols, local_channels = features.shape
    tiles_y, tiles_x = tissue.shape
    tiles = tiles_y * tiles_x
    channels = up_weight.shape[0]
    tp_index = lax.axis_index("tp")
    first = tp_index == 0
    channel_start = tp_index * local_channels
    other_start = (1 - tp_index) * local_channels
    contract_last = (((1,), (1,)), ((), ()))
    pixels = MOST * TILE * TILE

    down_t = lax.all_gather(down_weight.T, ("sy", "sx"), axis=0, tiled=True)

    flags = tissue.reshape(-1)
    tile_ids = jnp.arange(tiles, dtype=jnp.int32)
    earlier = (tile_ids[None, :] < tile_ids[:, None]).astype(jnp.int32)
    ahead = jnp.sum(earlier * flags[None, :], axis=1)
    slot_of = jnp.where(flags > 0, ahead, jnp.sum(flags) + tile_ids - ahead)
    chosen = [jnp.sum(jnp.where(slot_of == s, tile_ids, 0)) for s in range(MOST)]
    slot_mask = jnp.stack([jnp.sum(jnp.where(slot_of == s, flags, 0)) for s in range(MOST)])
    mask_rows = jnp.repeat(slot_mask, TILE * TILE).astype(jnp.float32)

    def windows_of(image, side):
        return jnp.stack(
            [
                lax.dynamic_slice(
                    image,
                    ((t // tiles_x) * TILE, (t % tiles_x) * TILE, 0),
                    (side, side, image.shape[2]),
                )
                for t in chosen
            ]
        )

    def spread_out(rows_array):
        held = rows_array.reshape(MOST, TILE, TILE, rows_array.shape[1])
        held = jnp.concatenate([held, jnp.zeros_like(held[:1])], axis=0)
        slots = jnp.minimum(slot_of, MOST)
        rows = []
        for ty in range(tiles_y):
            row = [
                lax.dynamic_index_in_dim(held, slots[ty * tiles_x + tx], 0, keepdims=False)
                for tx in range(tiles_x)
            ]
            rows.append(jnp.concatenate(row, axis=1))
        return jnp.concatenate(rows, axis=0)

    def both_halves(own):
        other = swapped(own)
        return jnp.where(
            first,
            jnp.concatenate([own, other], axis=1),
            jnp.concatenate([other, own], axis=1),
        )

    cot_tiles = windows_of(cotangent, TILE).reshape(pixels, local_channels)
    masked_cot = (cot_tiles.astype(jnp.float32) * mask_rows[:, None]).astype(jnp.bfloat16)
    cot_wide = both_halves(masked_cot)

    convolved = convolve(features, depth_kernel, depth_bias[None], False, 1)
    convolved = windows_of(convolved, TILE).reshape(pixels, local_channels)
    gathered = both_halves(convolved).astype(jnp.float32)
    centre = jnp.mean(gathered, axis=1, keepdims=True)
    spread = jnp.mean(jnp.square(gathered - centre), axis=1, keepdims=True)
    inv_scale = lax.rsqrt(spread + 1e-06)
    standard = (gathered - centre) * inv_scale
    normed = (standard * norm_gain + norm_bias).astype(jnp.bfloat16)
    preact = jnp.dot(normed, up_weight, preferred_element_type=jnp.float32) + up_bias
    hidden = gelu_value(preact).astype(jnp.bfloat16)
    hidden_wide = hidden.astype(jnp.float32)
    squares = jnp.sum(mask_rows[:, None] * hidden_wide * hidden_wide, axis=0)

    back_hidden = jnp.dot(cot_wide, down_t, preferred_element_type=jnp.float32)
    products = jnp.sum(back_hidden * hidden_wide, axis=0)
    scale, slope = response_scales(squares, products, response_gain)

    hidden_grad = back_hidden * scale + slope * mask_rows[:, None] * hidden_wide
    preact_grad = (hidden_grad * gelu_slope(preact)).astype(jnp.bfloat16)
    grad_terms = lax.dot_general(
        preact_grad, up_weight, contract_last, preferred_element_type=jnp.float32
    )
    scaled_terms = grad_terms * norm_gain
    sums_here = jnp.stack(
        [jnp.sum(scaled_terms, axis=1), jnp.sum(scaled_terms * standard, axis=1)]
    )
    sums = sums_here + swapped(sums_here)
    sent_grad = lax.dynamic_slice_in_dim(scaled_terms, other_start, local_channels, 1)
    kept_grad = lax.dynamic_slice_in_dim(scaled_terms, channel_start, local_channels, 1)
    own_standard = lax.dynamic_slice_in_dim(standard, channel_start, local_channels, 1)
    sent_grad, held_hidden = lax.optimization_barrier((sent_grad.astype(jnp.bfloat16), hidden))
    came_grad = swapped(sent_grad)
    response = (held_hidden.astype(jnp.float32) * scale + response_shift).astype(jnp.bfloat16)
    partial_out = lax.dot_general(
        response, down_t, contract_last, preferred_element_type=jnp.float32
    )
    sent_out = lax.dynamic_slice_in_dim(partial_out, other_start, local_channels, 1)
    kept_out = lax.dynamic_slice_in_dim(partial_out, channel_start, local_channels, 1)

    scaled = kept_grad + came_grad.astype(jnp.float32)
    convolved_grad = inv_scale * (
        scaled - (sums[0] / channels)[:, None] - own_standard * (sums[1] / channels)[:, None]
    )
    grad_image = spread_out(convolved_grad.astype(jnp.bfloat16))
    feature_grad, came_out = gradient_conv(
        grad_image, depth_kernel, cotangent, sent_out.astype(jnp.bfloat16)
    )
    branch = kept_out + came_out.astype(jnp.float32)

    addend = spread_out(mask_rows[:, None] * (branch + down_bias))
    block_out = (features.astype(jnp.float32) + addend).astype(jnp.bfloat16)
    return (block_out, feature_grad)


def solution(mesh):
    placed = (
        P("sy", "sx", "tp"),
        P(None, None, "tp"),
        P("tp"),
        P(),
        P(),
        P(None, "tp"),
        P("tp"),
        P("tp"),
        P("tp"),
        P("tp", ("sy", "sx")),
        P("tp"),
        P("sy", "sx"),
        P("sy", "sx", "tp"),
    )
    return jax.shard_map(
        shards,
        mesh=mesh,
        in_specs=placed,
        out_specs=(P("sy", "sx", "tp"), P("sy", "sx", "tp")),
        check_vma=False,
    )
```
